256 devices in a mesh: bx: 2 (over core), by: 4 (over z_lo), bz: 32 (over z_hi, y, x).
Axes of the slice: x: 4, y: 4, z: 8 (z_hi: 2, z_lo: 4; z = z_hi * 4 + z_lo), core: 2. Of those that a mesh axis runs over, the one named last changes fastest.
Arguments:
- skel_blocks: bfloat16 [2, 4, 32, 2, 256, 256], P('bx', 'by', 'bz'), may hold values from -6 to 6
- row_couple: bfloat16 [2, 4, 32, 27, 256, 256], P('bx', 'by', 'bz'), may hold values from -0.375 to 0.375
- col_couple: bfloat16 [2, 4, 32, 27, 256, 256], P('bx', 'by', 'bz'), may hold values from -0.375 to 0.375
- inverse_rr: bfloat16 [2, 4, 32, 256, 256], P('bx', 'by', 'bz'), may hold values from -0.0048828125 to 0.0048828125
- pivots: int32 [2, 4, 32, 256], P('bx', 'by', 'bz'), may hold values from 0 to 255, each once within a row
- self_block: float32 [2, 4, 32, 256, 256], P('bx', 'by', 'bz'), may hold values from -6 to 6
- skel_count: int32 [2, 4, 32], P('bx', 'by', 'bz'), may hold values from 64 to 256
- skel_order: int32 [2, 4, 32, 256], P('bx', 'by', 'bz'), may hold values from 0 to 255, each once within a row
- owner_flag: int32 [2, 4, 16], P('bx', 'by'), may hold values 0 or 1
Outputs:
- updated_self: float32 [2, 4, 32, 256, 256], P('bx', 'by', 'bz')
- parent_blocks: float32 [2, 4, 32, 2, 256, 256], P('bx', 'by', 'bz')
The draws below stay inside these ranges and needn't reach their ends.
Inputs may be any that keep to these rules, and one draw needn't show every extreme that they name: Each box's pivots are a permutation of 0 to 255. `skel_order`: each box's skeleton index list is a permutation of 0 to 255.
All inputs are finite; a program needn't handle non-finite values. No bound on the sum of `owner_flag` on one device may be relied on, other than what follows from the above.
Results may differ from the reference program's by a relative error of at most 0.0027.
Values may be sent and summed in bfloat16 or wider, within the bound.
No kernel may reach another device: no remote copies, remote signals or barrier semaphores. Data moves between devices by JAX's collectives and lax.ppermute only.
A program may use at most 64 MiB of HBM per device.

```python
import jax
import jax.numpy as jnp
from jax import lax

S = 256
R = 256
Q = 256
NBX = 2
NBY = 4
NBZ = 32


def with_ends(result, key, least, high):
    longest = result.shape.index(max(result.shape))
    spots = []
    for shift in (0, 1):
        where = [jax.random.randint(jax.random.fold_in(key, axis), (), 0, length) for axis, length in enumerate(result.shape)]
        where[longest] = (where[longest] + shift) % result.shape[longest]
        spots.append(tuple(where))
    return result.at[spots[0]].set(least).at[spots[1]].set(high)


def shard_levels(key, dims, pieces, smallest, largest):
    level, own = 1.0, jax.random.fold_in(key, 6)
    for axis_at, shards_of in pieces:
        heights = jnp.exp(jax.random.uniform(jax.random.fold_in(own, axis_at), (shards_of,), jnp.float32, smallest / len(pieces), largest / len(pieces)))
        level = level * jnp.repeat(heights, dims[axis_at] // shards_of).reshape([-1 if axis == axis_at else 1 for axis in range(len(dims))])
    return level


def gaussian(key, extent, width, bound, split=(), kind=jnp.bfloat16):
    gain = shard_levels(key, extent, split, -0.22, 0.18) if split else 1.0
    values = jax.random.normal(key, extent, jnp.float32) * width * gain
    return jnp.minimum(jnp.maximum(values, -bound), bound).astype(kind)


def setup_inputs(seed: int = 0) -> dict:
    key_of = jax.random.split(jax.random.key(seed), 10)
    skel_blocks = gaussian(key_of[0], (NBX, NBY, NBZ, 2, S, Q), 1.0, 6.0, ((0, 2), (1, 4), (2, 32)))
    row_couple = gaussian(key_of[1], (NBX, NBY, NBZ, 27, Q, R), Q ** -0.5, 0.375, ((0, 2), (1, 4), (2, 32)))
    col_couple = gaussian(key_of[2], (NBX, NBY, NBZ, 27, R, Q), Q ** -0.5, 0.375, ((0, 2), (1, 4), (2, 32)))
    inverse_rr = gaussian(key_of[3], (NBX, NBY, NBZ, R, R), (27 * R * R) ** -0.5, 0.0048828125, ((0, 2), (1, 4), (2, 32)))
    pivots = jax.vmap(lambda own: jax.random.permutation(own, R))(jax.random.split(key_of[4], NBX * NBY * NBZ)).reshape((NBX, NBY, NBZ, R)).astype(jnp.int32)
    self_block = gaussian(key_of[5], (NBX, NBY, NBZ, S, S), 1.0, 6.0, ((0, 2), (1, 4), (2, 32)), jnp.float32)
    skel_count = with_ends(jax.random.randint(key_of[6], (NBX, NBY, NBZ), S // 4, S + 1), jax.random.fold_in(key_of[6], 1), S // 4, S).astype(jnp.int32)
    skel_order = jax.vmap(lambda own: jax.random.permutation(own, S))(jax.random.split(key_of[7], NBX * NBY * NBZ)).reshape((NBX, NBY, NBZ, S)).astype(jnp.int32)
    owner_flag = with_ends((jax.random.randint(key_of[8], (NBX, NBY, NBZ // 2), 0, 2) < 1).astype(jnp.int32), jax.random.fold_in(key_of[8], 1), 0, 1)
    return dict(skel_blocks=skel_blocks, row_couple=row_couple, col_couple=col_couple, inverse_rr=inverse_rr, pivots=pivots, self_block=self_block, skel_count=skel_count, skel_order=skel_order, owner_flag=owner_flag)


def box_update(nearby, row_c, col_c, inverse, order):
    high = lax.Precision.HIGHEST
    rows = nearby[:, 0].astype(jnp.float32)
    cols = nearby[:, 1].astype(jnp.float32)
    upper = jnp.einsum('osq,oqr->osr', rows, row_c.astype(jnp.float32), precision=high).astype(jnp.bfloat16)
    lower = jnp.einsum('orq,osq->ors', col_c.astype(jnp.float32), cols, precision=high).astype(jnp.bfloat16)
    upper = lax.optimization_barrier(upper)
    lower = lax.optimization_barrier(lower)
    permuted = lower[:, order, :].astype(jnp.float32)
    solved = jnp.einsum('rk,oks->ors', inverse.astype(jnp.float32), permuted, precision=high).astype(jnp.bfloat16)
    solved = lax.optimization_barrier(solved)
    return jnp.einsum('osr,ort->ost', upper.astype(jnp.float32), solved.astype(jnp.float32), precision=high)


def reference(skel_blocks, row_couple, col_couple, inverse_rr, pivots, self_block, skel_count, skel_order, owner_flag):
    points = jnp.arange(S, dtype=jnp.int32)
    live = (points[None, None, None, :] < skel_count[..., None]).astype(jnp.bfloat16)
    masked = skel_blocks * live[:, :, :, None, :, None]
    padded = jnp.pad(masked, ((1, 1), (1, 1), (1, 1), (0, 0), (0, 0), (0, 0)))
    start = jnp.zeros((NBX + 2, NBY + 2, NBZ + 2, S, S), jnp.float32)
    zero = jnp.int32(0)

    def step(acc, index):
        xpos = (index // (NBY * NBZ)).astype(jnp.int32)
        ypos = ((index // NBZ) % NBY).astype(jnp.int32)
        zpos = (index % NBZ).astype(jnp.int32)
        nearby = lax.dynamic_slice(padded, (xpos, ypos, zpos, zero, zero, zero), (3, 3, 3, 2, S, Q)).reshape(27, 2, S, Q)
        piece = box_update(nearby, row_couple[xpos, ypos, zpos], col_couple[xpos, ypos, zpos], inverse_rr[xpos, ypos, zpos], pivots[xpos, ypos, zpos])
        piece = piece.reshape(3, 3, 3, S, S)
        current = lax.dynamic_slice(acc, (xpos, ypos, zpos, zero, zero), (3, 3, 3, S, S))
        acc = lax.dynamic_update_slice(acc, current + piece, (xpos, ypos, zpos, zero, zero))
        return acc, None

    acc, _ = lax.scan(step, start, jnp.arange(NBX * NBY * NBZ, dtype=jnp.int32))
    updated_self = self_block - acc[1:-1, 1:-1, 1:-1]

    def select(block, order, count):
        chosen = block[order][:, order]
        keep = (points[:, None] < count) & (points[None, :] < count)
        return jnp.where(keep, chosen, jnp.float32(0.0))

    flat = jax.vmap(select)(updated_self.reshape(-1, S, S), skel_order.reshape(-1, S), skel_count.reshape(-1))
    child = flat.reshape(NBX, NBY, NBZ // 2, 2, S, S)
    spread = jnp.repeat(child, 2, axis=2)
    owner = jnp.repeat(owner_flag, 2, axis=2)
    parity = (jnp.arange(NBZ, dtype=jnp.int32) % 2)[None, None, :]
    owns = (parity == owner)[:, :, :, None, None, None]
    parent_blocks = jnp.where(owns, spread, jnp.float32(0.0))
    return updated_self, parent_blocks
```

```python
import functools

import jax
import jax.numpy as jnp
from jax import lax
from jax.experimental import pallas as pl
from jax.experimental.pallas import tpu as pltpu
from jax.sharding import PartitionSpec as P

BF16 = jnp.bfloat16
F32 = jnp.float32
LIMIT = 16 * 1024 * 1024


def even_pairs(count):
    return [(i, i + 1) for i in range(0, count - 1, 2)]


def odd_pairs(count):
    return [(i, i + 1) for i in range(1, count - 1, 2)]


def swap(block, axis, pairs):
    route = []
    for low, high in pairs(lax.axis_size(axis)):
        route += [(low, high), (high, low)]
    return lax.ppermute(block, axis, route)


def dot(a, b):
    return jnp.dot(a, b, preferred_element_type=F32)


def dot_t(a, b):
    return lax.dot_general(a, b, (((1,), (1,)), ((), ())), preferred_element_type=F32)


def even_step(axis):
    return 1 - 2 * lax.rem(lax.axis_index(axis), 2)


def on_grid(axis, step):
    there = lax.axis_index(axis) + step
    return (there >= 0) & (there < lax.axis_size(axis))


def far_targets():
    y, z = even_step("by"), even_step("bz")
    return [(-z, y), (-z, -y), (-z, 0)]


def near_targets():
    y, z = even_step("by"), even_step("bz")
    return [(z, y), (z, -y), (z, 0), (0, y), (0, -y), (0, 0)]


def in_hbm(array):
    return pltpu.with_memory_space_constraint(array, pltpu.HBM)


def in_vmem(array):
    return pltpu.with_memory_space_constraint(array, pltpu.VMEM)


def call(kernel, inputs, outputs, scratch=(), flops=0, bytes_accessed=0, aliases=None):
    spaces = {"hbm": pltpu.HBM, "vmem": pltpu.VMEM, "smem": pltpu.SMEM}
    place = {"hbm": in_hbm, "vmem": in_vmem, "smem": lambda array: array}
    return pl.pallas_call(
        kernel,
        out_shape=tuple(outputs),
        in_specs=[pl.BlockSpec(memory_space=spaces[where]) for _, where in inputs],
        out_specs=tuple(
            pl.BlockSpec(memory_space=pltpu.HBM if isinstance(out, jax.ShapeDtypeStruct) else pltpu.VMEM)
            for out in outputs
        ),
        scratch_shapes=list(scratch),
        input_output_aliases=aliases or {},
        compiler_params=pltpu.CompilerParams(vmem_limit_bytes=LIMIT),
        cost_estimate=pl.CostEstimate(
            flops=flops, bytes_accessed=bytes_accessed, transcendentals=0
        ),
    )(*[place[where](array) for array, where in inputs])


def products(left, cols, start, order, store):
    size = cols.shape[1]
    for i, (z_step, y_step) in enumerate(order):
        inside = (on_grid("by", y_step) & on_grid("bz", z_step)).astype(F32)
        store(i, dot(left[i * size : (i + 1) * size], cols[start + i]) * inside)


def far_other_kernel(
    row_hbm, col_hbm, inverse_hbm, pivots_hbm, out, rows, cols, unpermuted, far_rows, far_cols, inverse, pivots, sems
):
    size = inverse.shape[0]
    other = even_step("bx")

    def place(x_step, step):
        z_step, y_step = step
        return 9 * (x_step + 1) + 3 * (y_step + 1) + (z_step + 1)

    def fetch(places, into_rows, into_cols, first):
        copies = []
        for i, at in enumerate(places):
            spot = into_rows.at[pl.ds(i * size, size), :]
            copies.append(
                (
                    pltpu.make_async_copy(row_hbm.at[at], spot, sems.at[0, first + i]),
                    pltpu.make_async_copy(col_hbm.at[at], into_cols.at[i], sems.at[1, first + i]),
                )
            )
        return copies

    head = [
        pltpu.make_async_copy(inverse_hbm, inverse, sems.at[0, 18]),
        pltpu.make_async_copy(pivots_hbm, pivots, sems.at[1, 18]),
    ]
    far = fetch([place(other, step) for step in far_targets()], far_rows, far_cols, 0)
    later = [place(other, step) for step in near_targets()]
    later += [place(0, step) for step in far_targets() + near_targets()]
    rest = fetch(later, rows, cols, 3)
    for copy in head:
        copy.start()
    for row_copy, _ in far:
        row_copy.start()
    for _, col_copy in far:
        col_copy.start()
    for row_copy, col_copy in rest:
        row_copy.start()
        col_copy.start()
    for copy in head:
        copy.wait()
    ids = lax.broadcasted_iota(jnp.int32, (size, size), 0)
    hot = (ids == pivots[...]).astype(F32).astype(BF16)
    unpermuted[...] = dot_t(inverse[...], hot).astype(BF16)
    for row_copy, _ in far:
        row_copy.wait()
    left = dot(far_rows[...], unpermuted[...]).astype(BF16)
    for _, col_copy in far:
        col_copy.wait()

    def store(i, value):
        out[i] = value.astype(BF16)

    products(left, far_cols, 0, far_targets(), store)
    for row_copy, col_copy in rest:
        row_copy.wait()
        col_copy.wait()


def near_other_kernel(rows, cols, unpermuted, out):
    left = dot(rows[0 : 6 * cols.shape[1], :], unpermuted[...]).astype(BF16)

    def store(i, value):
        out[i] = value.astype(BF16)

    products(left, cols, 0, near_targets(), store)


def own_kernel(rows, cols, unpermuted, far, near):
    left = dot(rows[6 * cols.shape[1] :, :], unpermuted[...]).astype(BF16)

    def store(i, value):
        if i < 3:
            far[i] = value
        else:
            near[i - 3] = value

    products(left, cols, 6, far_targets() + near_targets(), store)


def far_join_kernel(own, other, even, odd, keep):
    even[...] = (own[0] + other[0].astype(F32)).astype(BF16)
    odd[...] = (own[1] + other[1].astype(F32)).astype(BF16)
    keep[...] = own[2] + other[2].astype(F32)


def near_join_kernel(own, other, after, out, keep):
    del after
    out[...] = (own[0:3] + other[0:3].astype(F32)).astype(BF16)
    keep[...] = own[3:6] + other[3:6].astype(F32)


def far_kernel(keep, even, odd, out):
    out[...] = (keep[...] + even[...].astype(F32) + odd[...].astype(F32)).astype(BF16)


def near_kernel(center, side, even, odd, keep):
    total = center[...] + side[...].astype(F32)
    even[...] = total[0].astype(BF16)
    odd[...] = total[1].astype(BF16)
    keep[...] = total[2]


def select_kernel(
    count_ref, skel_hbm, order_hbm, self_hbm, rows_out, cols_out, chosen_out, self_vmem, skel, order, sems
):
    copies = [
        pltpu.make_async_copy(skel_hbm, skel, sems.at[0]),
        pltpu.make_async_copy(order_hbm, order, sems.at[1]),
        pltpu.make_async_copy(self_hbm, self_vmem, sems.at[2]),
    ]
    for copy in copies:
        copy.start()
    size = self_vmem.shape[0]
    count = count_ref[0]
    points = lax.broadcasted_iota(jnp.int32, (size, size), 0)
    lanes = lax.broadcasted_iota(jnp.int32, (size, size), 1)
    live = (points < count).astype(F32)
    for copy in copies:
        copy.wait()
    rows = (skel[0].astype(F32) * live).astype(BF16)
    cols = (skel[1].astype(F32) * live).astype(BF16)
    hot_t = ((points == order[...]) & (lanes < count)).astype(F32)
    hot = hot_t.T.astype(BF16)
    hot_t = hot_t.astype(BF16)

    def parts(value):
        high = value.astype(BF16)
        rest = value - high.astype(F32)
        middle = rest.astype(BF16)
        return high, middle, (rest - middle.astype(F32)).astype(BF16)

    high, middle, low = parts(self_vmem[...])
    picked = dot(hot, jnp.concatenate([rows, cols, high, middle, low], axis=1))
    rows_out[0:size, :] = rows
    rows_out[size:, :] = picked[:, :size].astype(BF16)
    cols_out[0] = cols
    cols_out[1] = picked[:, size : 2 * size].astype(BF16)
    by_row = (
        picked[:, 2 * size : 3 * size] + picked[:, 3 * size : 4 * size] + picked[:, 4 * size :]
    )
    both = dot(jnp.concatenate(parts(by_row), axis=0), hot_t)
    chosen_out[...] = both[:size] + both[size : 2 * size] + both[2 * size :]


def child_kernel(kept, even, odd, far, rows, cols, chosen, total_out, child, child_sent):
    size = chosen.shape[0]
    total = kept[...] + even[...].astype(F32) + odd[...].astype(F32) + far[...].astype(F32)
    total = total.astype(BF16)
    total_out[...] = total
    left = dot(rows[size:, :], total).astype(BF16)
    picked = chosen[...] - dot_t(left, cols[1])
    child[...] = picked
    child_sent[...] = picked.astype(BF16)


def owner_of_pair(owner):
    zpos = lax.axis_index("bz")
    parity = lax.rem(zpos, 2)
    return parity, (owner[0, 0, lax.div(zpos, 2)] == parity).astype(F32)


def update_kernel(owner, total, rows, cols, own_self, child, updated_hbm, parent_hbm, updated, mine, sems):
    size = own_self.shape[0]
    parity, owns = owner_of_pair(owner)
    mine[...] = child[...] * owns
    first = pltpu.make_async_copy(mine, parent_hbm.at[parity], sems.at[0])
    first.start()
    left = dot(rows[0:size, :], total[...]).astype(BF16)
    updated[...] = own_self[...] - dot_t(left, cols[0])
    second = pltpu.make_async_copy(updated, updated_hbm, sems.at[1])
    second.start()
    first.wait()
    second.wait()


def parent_kernel(owner, partner, parent_in, parent_hbm, theirs, sem):
    del parent_in
    parity, owns = owner_of_pair(owner)
    theirs[...] = partner[...].astype(F32) * owns
    copy = pltpu.make_async_copy(theirs, parent_hbm.at[1 - parity], sem)
    copy.start()
    copy.wait()


def on_device(
    skel_blocks,
    row_couple,
    col_couple,
    inverse_rr,
    pivots,
    self_block,
    skel_count,
    skel_order,
    owner_flag,
):
    size = inverse_rr.shape[-1]
    block = (size, size)
    row_couple = row_couple.reshape(row_couple.shape[-3:])
    col_couple = col_couple.reshape(col_couple.shape[-3:])
    inverse = inverse_rr.reshape(block)
    pivots = pivots.reshape(1, size)

    far_other, later_rows, later_cols, unpermuted = call(
        far_other_kernel,
        [(row_couple, "hbm"), (col_couple, "hbm"), (inverse, "hbm"), (pivots, "hbm")],
        [
            pltpu.VMEM((3, *block), BF16),
            pltpu.VMEM((15 * size, size), BF16),
            pltpu.VMEM((15, *block), BF16),
            pltpu.VMEM(block, BF16),
        ],
        [
            pltpu.VMEM((3 * size, size), BF16),
            pltpu.VMEM((3, *block), BF16),
            pltpu.VMEM(block, BF16),
            pltpu.VMEM((1, size), jnp.int32),
            pltpu.SemaphoreType.DMA((2, 19)),
        ],
        flops=14 * size**3,
        bytes_accessed=36 * 2 * size * size,
    )
    far_other = swap(far_other, "bx", even_pairs)
    later = [(later_rows, "vmem"), (later_cols, "vmem"), (unpermuted, "vmem")]
    (near_other,) = call(
        near_other_kernel,
        later,
        [pltpu.VMEM((6, *block), BF16)],
        flops=24 * size**3,
        bytes_accessed=36 * size * size,
    )
    near_other = swap(near_other, "bx", even_pairs)
    far_own, near_own = call(
        own_kernel,
        later,
        [pltpu.VMEM((3, *block), F32), pltpu.VMEM((6, *block), F32)],
        flops=36 * size**3,
        bytes_accessed=72 * size * size,
    )
    far_even, far_odd, far_keep = call(
        far_join_kernel,
        [(far_own, "vmem"), (far_other, "vmem")],
        [pltpu.VMEM(block, BF16), pltpu.VMEM(block, BF16), pltpu.VMEM(block, F32)],
        flops=3 * size * size,
        bytes_accessed=26 * size * size,
    )
    far_even = swap(far_even, "by", even_pairs)
    far_odd = swap(far_odd, "by", odd_pairs)
    side, center = call(
        near_join_kernel,
        [(near_own, "vmem"), (near_other, "vmem"), (far_keep, "vmem")],
        [pltpu.VMEM((3, *block), BF16), pltpu.VMEM((3, *block), F32)],
        flops=6 * size * size,
        bytes_accessed=54 * size * size,
    )
    side = swap(side, "bz", even_pairs)

    rows, cols, chosen, own_self = call(
        select_kernel,
        [
            (skel_count.reshape(1), "smem"),
            (skel_blocks.reshape(2, size, size), "hbm"),
            (skel_order.reshape(1, size), "hbm"),
            (self_block.reshape(block), "hbm"),
        ],
        [
            pltpu.VMEM((2 * size, size), BF16),
            pltpu.VMEM((2, size, size), BF16),
            pltpu.VMEM(block, F32),
            pltpu.VMEM(block, F32),
        ],
        [
            pltpu.VMEM((2, size, size), BF16),
            pltpu.VMEM((1, size), jnp.int32),
            pltpu.SemaphoreType.DMA((3,)),
        ],
        flops=16 * size**3,
        bytes_accessed=20 * size * size,
    )

    (far,) = call(
        far_kernel,
        [(far_keep, "vmem"), (far_even, "vmem"), (far_odd, "vmem")],
        [pltpu.VMEM(block, BF16)],
        flops=2 * size * size,
        bytes_accessed=10 * size * size,
    )
    far = swap(far, "bz", odd_pairs)
    near_even, near_odd, kept = call(
        near_kernel,
        [(center, "vmem"), (side, "vmem")],
        [pltpu.VMEM(block, BF16), pltpu.VMEM(block, BF16), pltpu.VMEM(block, F32)],
        flops=3 * size * size,
        bytes_accessed=26 * size * size,
    )
    near_even = swap(near_even, "by", even_pairs)
    near_odd = swap(near_odd, "by", odd_pairs)

    total, child, child_sent = call(
        child_kernel,
        [
            (kept, "vmem"),
            (near_even, "vmem"),
            (near_odd, "vmem"),
            (far, "vmem"),
            (rows, "vmem"),
            (cols, "vmem"),
            (chosen, "vmem"),
        ],
        [pltpu.VMEM(block, BF16), pltpu.VMEM(block, F32), pltpu.VMEM(block, BF16)],
        flops=4 * size**3,
        bytes_accessed=28 * size * size,
    )
    partner = swap(child_sent, "bz", even_pairs)
    updated, parent = call(
        update_kernel,
        [
            (owner_flag, "smem"),
            (total, "vmem"),
            (rows, "vmem"),
            (cols, "vmem"),
            (own_self, "vmem"),
            (child, "vmem"),
        ],
        [jax.ShapeDtypeStruct(block, F32), jax.ShapeDtypeStruct((2, *block), F32)],
        [pltpu.VMEM(block, F32), pltpu.VMEM(block, F32), pltpu.SemaphoreType.DMA((2,))],
        flops=4 * size**3,
        bytes_accessed=28 * size * size,
    )
    (parent,) = call(
        parent_kernel,
        [(owner_flag, "smem"), (partner, "vmem"), (parent, "hbm")],
        [jax.ShapeDtypeStruct((2, *block), F32)],
        [pltpu.VMEM(block, F32), pltpu.SemaphoreType.DMA],
        flops=size * size,
        bytes_accessed=6 * size * size,
        aliases={2: 0},
    )
    return (updated[None, None, None], parent[None, None, None])


def solution(mesh):
    in_specs = (
        P("bx", "by", "bz", None, None, None),
        P("bx", "by", "bz", None, None, None),
        P("bx", "by", "bz", None, None, None),
        P("bx", "by", "bz", None, None),
        P("bx", "by", "bz", None),
        P("bx", "by", "bz", None, None),
        P("bx", "by", "bz"),
        P("bx", "by", "bz", None),
        P("bx", "by", None),
    )
    out_specs = (P("bx", "by", "bz", None, None), P("bx", "by", "bz", None, None, None))
    return jax.shard_map(
        on_device, mesh=mesh, in_specs=in_specs, out_specs=out_specs, check_vma=False
    )
```

```python
import functools

import jax
import jax.numpy as jnp
from jax import lax
from jax.experimental import pallas as pl
from jax.experimental.pallas import tpu as pltpu
from jax.sharding import PartitionSpec as P

BF16 = jnp.bfloat16
F32 = jnp.float32
LIMIT = 16 * 1024 * 1024
HINT = 20 * 10**9


def swap_x(block):
    return lax.ppermute(block, "bx", [(0, 1), (1, 0)])


def swap_even(block, axis):
    route = []
    for low in range(0, lax.axis_size(axis) - 1, 2):
        route += [(low, low + 1), (low + 1, low)]
    return lax.ppermute(block, axis, route)


def swap_odd(block, axis):
    count = lax.axis_size(axis)
    route = []
    for x in (0, 1):
        for low in range(1, count - 1, 2):
            here, there = x * count + low, x * count + low + 1
            route += [(here, there), (there, here)]
        for end in (0, count - 1):
            route.append((x * count + end, (1 - x) * count + end))
    return lax.ppermute(block, ("bx", axis), route)


def swap_y(blocks):
    count = lax.axis_size("by")
    out = []
    for low, block in enumerate(blocks):
        route = []
        for x in (0, 1):
            for y in range(count):
                if y == low:
                    there = (x, y + 1)
                elif y == low + 1:
                    there = (x, y - 1)
                else:
                    there = (1 - x, y)
                route.append((x * count + y, there[0] * count + there[1]))
        out.append(lax.ppermute(block, ("bx", "by"), route))
    return out


def toward(pair):
    return jnp.where(lax.axis_index("by") == pair, 2, 0)


def received(pair, block):
    y = lax.axis_index("by")
    return block.astype(F32) * ((y == pair) | (y == pair + 1)).astype(F32)


def dot(a, b):
    return jnp.dot(a, b, preferred_element_type=F32)


def dot_t(a, b):
    return lax.dot_general(a, b, (((1,), (1,)), ((), ())), preferred_element_type=F32)


def even_step(axis):
    return 1 - 2 * lax.rem(lax.axis_index(axis), 2)


def on_grid(axis, step):
    there = lax.axis_index(axis) + step
    return (there >= 0) & (there < lax.axis_size(axis))


def in_hbm(array):
    return pltpu.with_memory_space_constraint(array, pltpu.HBM)


def in_vmem(array):
    return pltpu.with_memory_space_constraint(array, pltpu.VMEM)


def call(kernel, inputs, outputs, scratch=(), aliases=None, hint=0):
    spaces = {"hbm": pltpu.HBM, "vmem": pltpu.VMEM, "smem": pltpu.SMEM}
    place = {"hbm": in_hbm, "vmem": in_vmem, "smem": lambda array: array}
    return pl.pallas_call(
        kernel,
        out_shape=tuple(outputs),
        in_specs=[pl.BlockSpec(memory_space=spaces[where]) for _, where in inputs],
        out_specs=tuple(
            pl.BlockSpec(memory_space=pltpu.HBM if isinstance(out, jax.ShapeDtypeStruct) else pltpu.VMEM)
            for out in outputs
        ),
        scratch_shapes=list(scratch),
        input_output_aliases=aliases or {},
        compiler_params=pltpu.CompilerParams(vmem_limit_bytes=LIMIT),
        cost_estimate=pl.CostEstimate(
            flops=hint, bytes_accessed=0, transcendentals=0
        ),
    )(*[place[where](array) for array, where in inputs])


def z_steps():
    z = even_step("bz")
    return -z, z, 0


def products(rows, cols, unpermuted, steps, store):
    size = unpermuted.shape[0]
    count = 3 * len(steps)
    left = dot(rows.reshape(count * size, size), unpermuted).astype(BF16)
    for i in range(count):
        inside = on_grid("bz", steps[i // 3]).astype(F32)
        store(i, dot(left[i * size : (i + 1) * size], cols[i]) * inside)


def fetch(row_hbm, col_hbm, x, z, rows, cols, sems, at):
    return (
        pltpu.make_async_copy(row_hbm.at[x + 1, :, z + 1], rows, sems.at[0, at]),
        pltpu.make_async_copy(col_hbm.at[x + 1, :, z + 1], cols, sems.at[1, at]),
    )


def first_kernel(
    row_hbm, col_hbm, inverse_hbm, pivots_hbm, other, own, rows, cols, own_rows, own_cols, unpermuted, far_rows, far_cols, inverse, pivots, sems
):
    size = inverse.shape[0]
    x_step = even_step("bx")
    far, near, center = z_steps()
    low, high = pl.ds(0, 3), pl.ds(3, 3)
    head = (
        pltpu.make_async_copy(inverse_hbm, inverse, sems.at[0, 6]),
        pltpu.make_async_copy(pivots_hbm, pivots, sems.at[1, 6]),
    )
    far_other = fetch(row_hbm, col_hbm, x_step, far, far_rows.at[low], far_cols.at[low], sems, 0)
    far_own = fetch(row_hbm, col_hbm, 0, far, far_rows.at[high], far_cols.at[high], sems, 1)
    rest = fetch(row_hbm, col_hbm, x_step, near, rows.at[low], cols.at[low], sems, 2)
    rest += fetch(row_hbm, col_hbm, x_step, center, rows.at[high], cols.at[high], sems, 3)
    rest += fetch(row_hbm, col_hbm, 0, near, own_rows, own_cols, sems, 4)
    for copy in head + far_other + far_own + rest:
        copy.start()
    for copy in head:
        copy.wait()
    ids = lax.broadcasted_iota(jnp.int32, (size, size), 0)
    hot = (ids == pivots[...]).astype(F32).astype(BF16)
    unpermuted[...] = dot_t(inverse[...], hot).astype(BF16)

    def store_other(i, value):
        other[i] = value.astype(BF16)

    def store_own(i, value):
        own[i] = value

    for copy in far_other:
        copy.wait()
    products(far_rows[0:3], far_cols.at[low], unpermuted[...], [far], store_other)
    for copy in far_own:
        copy.wait()
    products(far_rows[3:6], far_cols.at[high], unpermuted[...], [far], store_own)
    for copy in rest:
        copy.wait()


def near_other_kernel(row_hbm, col_hbm, rows, cols, unpermuted, out, center_rows, center_cols, sems):
    copies = fetch(row_hbm, col_hbm, 0, 0, center_rows, center_cols, sems, 0)
    for copy in copies:
        copy.start()

    def store(i, value):
        out[i] = value.astype(BF16)

    products(rows[...], cols, unpermuted[...], z_steps()[1:], store)
    for copy in copies:
        copy.wait()


def far_join_kernel(own, other, first, second, third, keep):
    for pair, out in enumerate((first, second, third)):
        at = toward(pair)
        out[...] = (own[at] + other[at].astype(F32)).astype(BF16)
    keep[...] = own[1] + other[1].astype(F32)


def near_join_kernel(rows, cols, center_rows, center_cols, unpermuted, other, after, outer, middle, center):
    del after

    def store(i, value):
        total = value + other[i].astype(F32)
        if i == 1:
            middle[...] = total.astype(BF16)
        elif i < 3:
            outer[i // 2] = total.astype(BF16)
        else:
            center[i - 3] = total

    products(rows[...], cols, unpermuted[...], z_steps()[1:2], store)
    products(center_rows[...], center_cols, unpermuted[...], z_steps()[2:], lambda i, value: store(i + 3, value))


def far_kernel(keep, first, second, third, out):
    total = keep[...]
    for pair, block in enumerate((first, second, third)):
        total += received(pair, block[...])
    out[...] = total.astype(BF16)


def near_kernel(center, outer, after, first, second, third):
    del after
    for pair, out in enumerate((first, second, third)):
        at = toward(pair)
        out[...] = (center[at] + outer[at // 2].astype(F32)).astype(BF16)


def select_kernel(
    count_ref, skel_hbm, order_hbm, self_hbm, near_middle, after, rows_out, cols_out, chosen_out, self_vmem, extra_out, skel, order, sems
):
    del after
    copies = [
        pltpu.make_async_copy(skel_hbm, skel, sems.at[0]),
        pltpu.make_async_copy(order_hbm, order, sems.at[1]),
        pltpu.make_async_copy(self_hbm, self_vmem, sems.at[2]),
    ]
    for copy in copies:
        copy.start()
    size = self_vmem.shape[0]
    count = count_ref[0]
    points = lax.broadcasted_iota(jnp.int32, (size, size), 0)
    lanes = lax.broadcasted_iota(jnp.int32, (size, size), 1)
    live = (points < count).astype(F32)
    for copy in copies:
        copy.wait()
    rows = (skel[0].astype(F32) * live).astype(BF16)
    cols = (skel[1].astype(F32) * live).astype(BF16)
    hot_t = ((points == order[...]) & (lanes < count)).astype(F32)
    hot = hot_t.T.astype(BF16)
    hot_t = hot_t.astype(BF16)

    def parts(value):
        high = value.astype(BF16)
        rest = value - high.astype(F32)
        middle = rest.astype(BF16)
        return high, middle, (rest - middle.astype(F32)).astype(BF16)

    high, middle, low = parts(self_vmem[...])
    picked = dot(hot, jnp.concatenate([rows, cols, high, middle, low], axis=1))
    rows_out[0:size, :] = rows
    rows_out[size:, :] = picked[:, :size].astype(BF16)
    cols_out[0] = cols
    cols_out[1] = picked[:, size : 2 * size].astype(BF16)
    by_row = (
        picked[:, 2 * size : 3 * size] + picked[:, 3 * size : 4 * size] + picked[:, 4 * size :]
    )
    both = dot(jnp.concatenate(parts(by_row), axis=0), hot_t)
    chosen = both[:size] + both[size : 2 * size] + both[2 * size :]
    chosen_out[...] = chosen
    extra_out[0] = near_middle[...]
    extra_out[1] = chosen.astype(BF16)


def halves(value):
    high = value.astype(BF16)
    return high, (value - high.astype(F32)).astype(BF16)


def change(rows, total, cols):
    high, low = total[0], total[1]
    left_high, left_low = halves(dot(rows, high) + dot(rows, low))
    return dot_t(left_high, cols) + dot_t(left_low, cols)


def child_kernel(center, extra, first, second, third, far, rows, cols, chosen, total, child, child_sent):
    size = chosen.shape[0]
    value = center[1] + extra[0].astype(F32)
    for pair, block in enumerate((first, second, third)):
        value += received(pair, block[...])
    high, low = halves(value + far[...].astype(F32))
    total[0] = high
    total[1] = low
    less = change(rows[size:, :], total, cols[1])
    child[...] = chosen[...] - less
    child_sent[...] = (less - (chosen[...] - chosen[...].astype(BF16).astype(F32))).astype(BF16)


def update_kernel(owner, total, rows, cols, own_self, child, updated_hbm, parent_hbm, updated, mine, sems):
    size = own_self.shape[0]
    zpos = lax.axis_index("bz")
    parity = lax.rem(zpos, 2)
    mine[...] = child[...] * (owner[0, 0, lax.div(zpos, 2)] == parity).astype(F32)
    first = pltpu.make_async_copy(mine, parent_hbm.at[parity], sems.at[0])
    first.start()
    updated[...] = own_self[...] - change(rows[0:size, :], total, cols[0])
    second = pltpu.make_async_copy(updated, updated_hbm, sems.at[1])
    second.start()
    first.wait()
    second.wait()


def on_device(
    skel_blocks,
    row_couple,
    col_couple,
    inverse_rr,
    pivots,
    self_block,
    skel_count,
    skel_order,
    owner_flag,
):
    size = inverse_rr.shape[-1]
    block = (size, size)
    row_couple = row_couple.reshape(3, 3, 3, size, size)
    col_couple = col_couple.reshape(3, 3, 3, size, size)
    inverse = inverse_rr.reshape(block)
    pivots = pivots.reshape(1, size)

    far_other, far_own, other_rows, other_cols, own_rows, own_cols, unpermuted = call(
        first_kernel,
        [(row_couple, "hbm"), (col_couple, "hbm"), (inverse, "hbm"), (pivots, "hbm")],
        [
            pltpu.VMEM((3, *block), BF16),
            pltpu.VMEM((3, *block), F32),
            pltpu.VMEM((6, *block), BF16),
            pltpu.VMEM((6, *block), BF16),
            pltpu.VMEM((3, *block), BF16),
            pltpu.VMEM((3, *block), BF16),
            pltpu.VMEM(block, BF16),
        ],
        [
            pltpu.VMEM((6, *block), BF16),
            pltpu.VMEM((6, *block), BF16),
            pltpu.VMEM(block, BF16),
            pltpu.VMEM((1, size), jnp.int32),
            pltpu.SemaphoreType.DMA((2, 7)),
        ],
    )
    far_other = swap_x(far_other)
    near_other, center_rows, center_cols = call(
        near_other_kernel,
        [
            (row_couple, "hbm"),
            (col_couple, "hbm"),
            (other_rows, "vmem"),
            (other_cols, "vmem"),
            (unpermuted, "vmem"),
        ],
        [pltpu.VMEM((6, *block), BF16), pltpu.VMEM((3, *block), BF16), pltpu.VMEM((3, *block), BF16)],
        [pltpu.SemaphoreType.DMA((2, 1))],
    )
    near_other = swap_x(near_other)
    *far_sides, far_keep = call(
        far_join_kernel,
        [(far_own, "vmem"), (far_other, "vmem")],
        [pltpu.VMEM(block, BF16)] * 3 + [pltpu.VMEM(block, F32)],
        hint=HINT,
    )
    far_sides = swap_y(far_sides)
    outer, middle, center = call(
        near_join_kernel,
        [
            (own_rows, "vmem"),
            (own_cols, "vmem"),
            (center_rows, "vmem"),
            (center_cols, "vmem"),
            (unpermuted, "vmem"),
            (near_other, "vmem"),
            (far_keep, "vmem"),
        ],
        [pltpu.VMEM((2, *block), BF16), pltpu.VMEM(block, BF16), pltpu.VMEM((3, *block), F32)],
    )
    outer = swap_even(outer, "bz")
    (far,) = call(
        far_kernel,
        [(far_keep, "vmem")] + [(side, "vmem") for side in far_sides],
        [pltpu.VMEM(block, BF16)],
        hint=HINT,
    )
    far_sent = far
    far = swap_odd(far, "bz")

    rows, cols, chosen, own_self, extra = call(
        select_kernel,
        [
            (skel_count.reshape(1), "smem"),
            (skel_blocks.reshape(2, size, size), "hbm"),
            (skel_order.reshape(1, size), "hbm"),
            (self_block.reshape(block), "hbm"),
            (middle, "vmem"),
            (far_sent, "vmem"),
        ],
        [
            pltpu.VMEM((2 * size, size), BF16),
            pltpu.VMEM((2, size, size), BF16),
            pltpu.VMEM(block, F32),
            pltpu.VMEM(block, F32),
            pltpu.VMEM((2, *block), BF16),
        ],
        [
            pltpu.VMEM((2, size, size), BF16),
            pltpu.VMEM((1, size), jnp.int32),
            pltpu.SemaphoreType.DMA((3,)),
        ],
    )
    extra = swap_even(extra, "bz")
    near_sides = call(
        near_kernel,
        [(center, "vmem"), (outer, "vmem"), (chosen, "vmem")],
        [pltpu.VMEM(block, BF16)] * 3,
        hint=HINT,
    )
    near_sides = swap_y(near_sides)

    total, child, child_sent = call(
        child_kernel,
        [
            (center, "vmem"),
            (extra, "vmem"),
            *[(side, "vmem") for side in near_sides],
            (far, "vmem"),
            (rows, "vmem"),
            (cols, "vmem"),
            (chosen, "vmem"),
        ],
        [pltpu.VMEM((2, *block), BF16), pltpu.VMEM(block, F32), pltpu.VMEM(block, BF16)],
    )
    partner = swap_even(child_sent, "bz")
    updated, parent = call(
        update_kernel,
        [
            (owner_flag, "smem"),
            (total, "vmem"),
            (rows, "vmem"),
            (cols, "vmem"),
            (own_self, "vmem"),
            (child, "vmem"),
        ],
        [jax.ShapeDtypeStruct(block, F32), jax.ShapeDtypeStruct((2, *block), F32)],
        [pltpu.VMEM(block, F32), pltpu.VMEM(block, F32), pltpu.SemaphoreType.DMA((2,))],
    )
    zpos = lax.axis_index("bz")
    parity = zpos % 2
    flag = lax.dynamic_index_in_dim(owner_flag[0, 0], zpos // 2, 0, keepdims=False)
    theirs = extra[1].astype(F32) - partner.astype(F32)
    theirs = jnp.where(parity == flag, theirs, F32(0.0))
    parent = lax.dynamic_update_index_in_dim(parent, theirs, 1 - parity, 0)
    return (updated[None, None, None], parent[None, None, None])


def solution(mesh):
    in_specs = (
        P("bx", "by", "bz", None, None, None),
        P("bx", "by", "bz", None, None, None),
        P("bx", "by", "bz", None, None, None),
        P("bx", "by", "bz", None, None),
        P("bx", "by", "bz", None),
        P("bx", "by", "bz", None, None),
        P("bx", "by", "bz"),
        P("bx", "by", "bz", None),
        P("bx", "by", None),
    )
    out_specs = (P("bx", "by", "bz", None, None), P("bx", "by", "bz", None, None, None))
    return jax.shard_map(
        on_device, mesh=mesh, in_specs=in_specs, out_specs=out_specs, check_vma=False
    )
```
